32 devices in a mesh: grp: 2 (over y), inst: 4 (over z), tp: 4 (over x, core).
Axes of the slice: x: 2, y: 2, z: 4, core: 2. Of those that a mesh axis runs over, the one named last changes fastest.
Arguments:
- pre_q: bfloat16 [6144, 8192], P(('grp', 'inst'), 'tp'), parts along dimension 0, may hold values from -60 to 60
- pre_kv: bfloat16 [6144, 2, 1024], P(('grp', 'inst'), None, 'tp'), parts along dimension 0, may hold values from -60 to 60
- prompt_len: int32 [8, 4], P(('grp', 'inst')), parts along dimension 0, may hold values from 1 to 384, 768 in all within a row
- page_owner: int32 [192, 1], P('grp'), parts along dimension 0, may hold values from 0 to 3; in each aligned block of 24 rows (0 to 23, 24 to 47, ...) at most 12 rows name the same one
- page_row: int32 [192], P('grp'), parts along dimension 0, may hold values from 0 to 3
- dec_q: bfloat16 [32, 4, 8192], P(('grp', 'inst'), None, 'tp'), parts along dimension 0, may hold values from -60 to 60
- dec_kv: bfloat16 [32, 4, 2, 1024], P(('grp', 'inst'), None, None, 'tp'), parts along dimension 0, may hold values from -60 to 60
- cache_kv: bfloat16 [32, 512, 2, 1024], P(('grp', 'inst'), None, None, 'tp'), parts along dimension 0, may hold values from -60 to 60
- cache_len: int32 [8, 4], P(('grp', 'inst')), parts along dimension 0, may hold values from 1 to 512, 1280 in all within a row
- w_out: bfloat16 [8192, 8192], P('tp', 'inst'), may hold values from -0.0625 to 0.0625
Outputs:
- prefill_out: bfloat16 [6144, 8192], P(('grp', 'inst'), 'tp'), parts along dimension 0
- decode_out: bfloat16 [128, 8192], P(('grp', 'tp'), 'inst'), parts along dimension 0
The draws below stay inside these ranges and needn't reach their ends.
There are 2 independent parts, one for each index of `grp`. The reference program is written for one: setup_inputs(seed, part) draws one part's arguments, and reference() takes and returns one part's arrays. A program takes and returns all parts, laid end to end along the dimension named above; an argument that names none is the same for every part. Nothing has to cross between parts.
Inputs may be any that keep to these rules, and one draw needn't show every extreme that they name: `prompt_len`: on every instance the 4 lengths sum to 768 and the longest is exactly 384. `page_owner`: no instance sends more than 12 of its pages to one owner; in every draw some instance sends exactly 12 pages to one owner. `cache_len`: on every owner the 4 lengths sum to 1280 and the longest is exactly 512.
All inputs are finite; a program needn't handle non-finite values.
Results may differ from the reference program's by a relative error of at most 0.005.
Values may be sent and summed in bfloat16 or wider, within the bound.
A program may use at most 128 MiB of HBM per device.

```python
import math
import jax
import jax.numpy as jnp
import numpy as np
from jax import lax

D = 8192
HEADS = 64
KV_HEADS = 8
HEAD_DIM = 128
BLK = 32
NPRE = 4
PTOK = 768
PMAX = 384
NPAGE = 24
MOSTP = 12
RDEV = 4
STEPS = 4
CAP = 512
ROWS = 16
N_INST = 4


def query_law(key, lead):
    noise = jax.random.normal(jax.random.fold_in(key, 1), lead + (HEADS, HEAD_DIM), jnp.float32)
    values = jnp.clip(noise, -60.0, 60.0)
    return values.reshape(lead + (HEADS * HEAD_DIM,)).astype(jnp.bfloat16)


def keyval_law(key, lead):
    noise = jax.random.normal(jax.random.fold_in(key, 3), lead + (KV_HEADS, HEAD_DIM), jnp.float32)
    key_part = jnp.clip(noise, -60.0, 60.0)
    value_part = jnp.clip(jax.random.normal(jax.random.fold_in(key, 5), lead + (KV_HEADS, HEAD_DIM), jnp.float32), -60.0, 60.0)
    stacked = jnp.stack([key_part, value_part], axis=len(lead))
    return stacked.reshape(lead + (2, KV_HEADS * HEAD_DIM)).astype(jnp.bfloat16)


def draw_pre_q(key, part):
    key = jax.random.fold_in(key, 11)
    return query_law(key, (N_INST * PTOK,))


def draw_pre_kv(key, part):
    key = jax.random.fold_in(key, 12)
    return keyval_law(key, (N_INST * PTOK,))


def draw_dec_q(key, part):
    key = jax.random.fold_in(key, 13)
    return query_law(key, (ROWS, STEPS))


def draw_dec_kv(key, part):
    key = jax.random.fold_in(key, 14)
    return keyval_law(key, (ROWS, STEPS))


def draw_cache_kv(key, part):
    key = jax.random.fold_in(key, 15)
    return keyval_law(key, (ROWS, CAP))


def set_ends(entries, rng, low, high):
    place = [jax.random.randint(jax.random.fold_in(rng, axis), (), 0, length) for axis, length in enumerate(entries.shape)]
    main_axis = entries.shape.index(max(entries.shape))
    neighbour = place[:main_axis] + [(place[main_axis] + 1) % entries.shape[main_axis]] + place[main_axis + 1:]
    return entries.at[tuple(place)].set(low).at[tuple(neighbour)].set(high)


def shard_levels(stream_key, dims, shards, low, high):
    def one(dim, parts):
        steps = jax.random.uniform(jax.random.fold_in(jax.random.fold_in(stream_key, 6), dim), (parts,), jnp.float32, low / len(shards), high / len(shards))
        return jnp.repeat(jnp.exp(steps), dims[dim] // parts).reshape((-1,) + (1,) * (len(dims) - dim - 1))

    level = one(*shards[0])
    for cut in shards[1:]:
        level = level * one(*cut)
    return level


def profile(number_of, total, reach, slope):
    portions = [(1 << 20) // math.isqrt(rank ** slope) + 1 for rank in range(2, number_of + 1)]
    spare, holding = total - reach - (number_of - 1), [1] * (number_of - 1)
    while spare > 0:
        movable = [i for i in range(number_of - 1) if holding[i] < reach]
        mass, left = sum([portions[i] for i in movable]), spare
        for i in movable:
            addition = min(reach - holding[i], max(1, left * portions[i] // mass), spare)
            holding[i] = holding[i] + addition
            spare = spare - addition
    return np.array([reach] + holding)


def uneven_parts(own_key, count, total, reach, lean):
    if count == 2:
        one = jax.random.randint(own_key, (), max(1, total - reach), min(reach, total - 1) + 1)
        return jnp.stack([one, total - one])
    sizes = jnp.asarray(profile(count, total, reach, lean), jnp.int32)
    couples = (count - 1) // 2
    source_of, sink = sizes[1:1 + 2 * couples:2], sizes[2:2 + 2 * couples:2]
    room = jnp.minimum(source_of - 1, reach - sink)
    moved = jax.random.randint(jax.random.fold_in(own_key, 1), (couples,), 0, 1 << 20) % (room + 1)
    sizes = sizes.at[1:1 + 2 * couples:2].set(source_of - moved).at[2:2 + 2 * couples:2].set(sink + moved)
    return sizes[jax.random.permutation(jax.random.fold_in(own_key, 2), count)]


def assign_block(key, own, number, rows, count, top, most, lean):
    sequence = jax.random.permutation(key, count)
    packed, ordinary = shares(count, rows * top, most, lean, True), shares(count, rows * top, most, lean, False)
    places = jnp.arange(count)

    def named(sizes, rotation):
        used = int((sizes > 0).sum())
        fixed = max(1, used // 4)
        passed = fixed + (places - fixed + rotation * (used - fixed)) % max(1, count - fixed)
        return jnp.zeros((count,), jnp.int32).at[sequence[jnp.where(places < fixed, places, passed)]].set(jnp.asarray(sizes, jnp.int32))

    sizes = jnp.where(number % 4 == 0, named(packed, number // 4), named(ordinary, number - number // 4 - 1))
    mixed = jax.random.permutation(jax.random.fold_in(own, 3), count)
    giver, taker = mixed[0:count // 2 * 2:2], mixed[1:count // 2 * 2:2]
    room = jnp.minimum(sizes[giver] - 1, most - sizes[taker]) // 2
    room = jnp.where((giver == sequence[0]) | (taker == sequence[0]) | (sizes[taker] == 0), 0, jnp.maximum(room, 0))
    passed = jax.random.randint(jax.random.fold_in(own, 4), (count // 2,), 0, 1 << 20) % (room + 1)
    sizes = sizes.at[giver].add(-passed).at[taker].add(passed)
    labels = jnp.searchsorted(jnp.cumsum(sizes), jnp.arange(rows * top), side="right").astype(jnp.int32)
    grid = labels.reshape(top, rows).T
    grid = grid[jax.random.permutation(jax.random.fold_in(own, 1), rows)]
    rotation = jax.random.randint(jax.random.fold_in(own, 2), (rows, 1), 0, top)
    return jnp.take_along_axis(grid, (jnp.arange(top)[None, :] + rotation) % top, axis=1)


def shares(number_of, total, reach, slope, full):
    portions = [(1 << 20) // math.isqrt(rank ** slope) + 1 for rank in range(1, number_of + 1)]
    largest = reach if full else min(reach, max(-(-total // number_of), total * portions[0] // sum(portions)))
    least = 1 if total - largest >= number_of - 1 else 0
    holding, rest = [largest] + [least] * (number_of - 1), total - largest - least * (number_of - 1)
    while rest > 0:
        free = [i for i in range(1, number_of) if holding[i] < largest] or [i for i in range(1, number_of) if holding[i] < reach]
        pool, left = sum([portions[i] for i in free]), rest
        for i in free:
            extra = min(reach - holding[i], max(1, left * portions[i] // pool), rest)
            holding[i] = holding[i] + extra
            rest = rest - extra
    return np.array(holding)


def scatter_about(stream_key, shape, spread, reach, pieces=(), held_as=jnp.bfloat16):
    factor_of = shard_levels(stream_key, shape, pieces, -0.22, 0.18) if pieces else 1.0
    result = jax.random.normal(stream_key, shape, jnp.float32) * spread * factor_of
    return jnp.minimum(jnp.maximum(result, -reach), reach).astype(held_as)


def setup_inputs(seed: int = 0, part: int = 0) -> dict:
    seeds = jax.random.split(jax.random.key(seed), 11)
    part_splits = jax.random.split(jax.random.fold_in(seeds[10], part), 11)
    pre_q = draw_pre_q(jax.random.fold_in(jax.random.fold_in(seeds[10], part), 71), part)
    pre_kv = draw_pre_kv(jax.random.fold_in(jax.random.fold_in(seeds[10], part), 71), part)
    prompt_len = jax.vmap(lambda own: uneven_parts(own, NPRE, PTOK, PMAX, 2))(jax.random.split(part_splits[2], N_INST)).reshape((N_INST, NPRE)).astype(jnp.int32)
    page_owner_keys = jax.random.split(jax.random.fold_in(part_splits[3], 1), (N_INST * NPAGE) // NPAGE)
    page_owner_turns = jax.random.permutation(jax.random.fold_in(part_splits[3], 3), (N_INST * NPAGE) // NPAGE)
    page_owner = jax.vmap(lambda own, number: assign_block(jax.random.fold_in(part_splits[3], 2), own, number, NPAGE, N_INST, 1, MOSTP, 2))(page_owner_keys, page_owner_turns).reshape((N_INST * NPAGE, 1))
    page_row = set_ends(jax.random.randint(part_splits[4], (N_INST * NPAGE,), 0, RDEV), jax.random.fold_in(part_splits[4], 1), 0, RDEV - 1).astype(jnp.int32)
    dec_q = draw_dec_q(jax.random.fold_in(jax.random.fold_in(seeds[10], part), 71), part)
    dec_kv = draw_dec_kv(jax.random.fold_in(jax.random.fold_in(seeds[10], part), 71), part)
    cache_kv = draw_cache_kv(jax.random.fold_in(jax.random.fold_in(seeds[10], part), 71), part)
    cache_len = jax.vmap(lambda own: uneven_parts(own, RDEV, RDEV * CAP * 5 // 8, CAP, 2))(jax.random.split(part_splits[8], N_INST)).reshape((N_INST, RDEV)).astype(jnp.int32)
    w_out = scatter_about(seeds[9], (HEADS * HEAD_DIM, D), (HEADS * HEAD_DIM) ** -0.5, 0.0625, ((0, 4), (1, 4)))
    return dict(pre_q=pre_q, pre_kv=pre_kv, prompt_len=prompt_len, page_owner=page_owner, page_row=page_row, dec_q=dec_q, dec_kv=dec_kv, cache_kv=cache_kv, cache_len=cache_len, w_out=w_out)


NEG_FILL = -1e30


def prefill_block(items):
    queries, keyvals, lengths = items
    per_group = HEADS // KV_HEADS
    prompt_ends = jnp.cumsum(lengths)
    position = jnp.arange(PTOK, dtype=jnp.int32)
    prompt_id = jnp.sum((position[:, None] >= prompt_ends[None, :]).astype(jnp.int32), axis=1)
    allowed = (prompt_id[:, None] == prompt_id[None, :]) & (position[:, None] >= position[None, :])
    query_heads = queries.astype(jnp.float32).reshape(PTOK, KV_HEADS, per_group, HEAD_DIM)
    key_rows = keyvals[:, 0].astype(jnp.float32).reshape(PTOK, KV_HEADS, HEAD_DIM)
    value_rows = keyvals[:, 1].astype(jnp.float32).reshape(PTOK, KV_HEADS, HEAD_DIM)
    scores = jnp.einsum("qigd,tid->igqt", query_heads, key_rows, precision=lax.Precision.HIGHEST) * (HEAD_DIM ** -0.5)
    scores = jnp.where(allowed[None, None], scores, NEG_FILL)
    weights = jax.nn.softmax(scores, axis=-1)
    weights = lax.optimization_barrier(weights.astype(jnp.bfloat16)).astype(jnp.float32)
    mixture = jnp.einsum("igqt,tid->qigd", weights, value_rows, precision=lax.Precision.HIGHEST)
    return mixture.reshape(PTOK, HEADS * HEAD_DIM).astype(jnp.bfloat16)


def reference(pre_q, pre_kv, prompt_len, page_owner, page_row, dec_q, dec_kv, cache_kv, cache_len, w_out):
    prefill_out = lax.map(prefill_block, (pre_q.reshape(N_INST, PTOK, HEADS * HEAD_DIM), pre_kv.reshape(N_INST, PTOK, 2, KV_HEADS * HEAD_DIM), prompt_len))
    prefill_out = prefill_out.reshape(N_INST * PTOK, HEADS * HEAD_DIM)
    per_group = HEADS // KV_HEADS
    pool_keys = pre_kv[:, 0].astype(jnp.float32).reshape(N_INST * PTOK, KV_HEADS, HEAD_DIM)
    pool_values = pre_kv[:, 1].astype(jnp.float32).reshape(N_INST * PTOK, KV_HEADS, HEAD_DIM)
    token_owner = jnp.repeat(page_owner[:, 0], BLK)
    token_row = jnp.repeat(page_row, BLK)
    scale_factor = HEAD_DIM ** -0.5
    step_index = jnp.arange(STEPS, dtype=jnp.int32)
    causal = step_index[None, :] <= step_index[:, None]
    slot_index = jnp.arange(CAP, dtype=jnp.int32)

    def decode_row(row_index):
        owner_index = row_index // RDEV
        local_row = row_index % RDEV
        query_heads = dec_q[row_index].astype(jnp.float32).reshape(STEPS, KV_HEADS, per_group, HEAD_DIM)
        cache_keys = cache_kv[row_index, :, 0].astype(jnp.float32).reshape(CAP, KV_HEADS, HEAD_DIM)
        cache_values = cache_kv[row_index, :, 1].astype(jnp.float32).reshape(CAP, KV_HEADS, HEAD_DIM)
        fresh_keys = dec_kv[row_index, :, 0].astype(jnp.float32).reshape(STEPS, KV_HEADS, HEAD_DIM)
        fresh_values = dec_kv[row_index, :, 1].astype(jnp.float32).reshape(STEPS, KV_HEADS, HEAD_DIM)
        cache_length = cache_len[owner_index, local_row]
        cache_scores = jnp.einsum("sigd,tid->sigt", query_heads, cache_keys, precision=lax.Precision.HIGHEST) * scale_factor
        cache_scores = jnp.where((slot_index < cache_length)[None, None, None, :], cache_scores, NEG_FILL)
        pool_scores = jnp.einsum("sigd,tid->sigt", query_heads, pool_keys, precision=lax.Precision.HIGHEST) * scale_factor
        pool_live = (token_owner == owner_index) & (token_row == local_row)
        pool_scores = jnp.where(pool_live[None, None, None, :], pool_scores, NEG_FILL)
        fresh_scores = jnp.einsum("sigd,tid->sigt", query_heads, fresh_keys, precision=lax.Precision.HIGHEST) * scale_factor
        fresh_scores = jnp.where(causal[:, None, None, :], fresh_scores, NEG_FILL)
        scores = jnp.concatenate([cache_scores, pool_scores, fresh_scores], axis=-1)
        weights = jax.nn.softmax(scores, axis=-1)
        mixture = jnp.einsum("sigt,tid->sigd", weights[..., :CAP], cache_values, precision=lax.Precision.HIGHEST)
        mixture = mixture + jnp.einsum("sigt,tid->sigd", weights[..., CAP:CAP + N_INST * PTOK], pool_values, precision=lax.Precision.HIGHEST)
        mixture = mixture + jnp.einsum("sigt,tid->sigd", weights[..., CAP + N_INST * PTOK:], fresh_values, precision=lax.Precision.HIGHEST)
        return mixture.reshape(STEPS, HEADS * HEAD_DIM).astype(jnp.bfloat16)

    attention = lax.map(decode_row, jnp.arange(ROWS, dtype=jnp.int32))
    decode_out = jnp.dot(attention.reshape(ROWS * STEPS, HEADS * HEAD_DIM), w_out, preferred_element_type=jnp.float32).astype(jnp.bfloat16)
    return prefill_out, decode_out
```

```python
import functools
import math

import jax
import jax.numpy as jnp
from jax import lax
from jax.experimental import pallas as pl
from jax.experimental.pallas import tpu as pltpu
from jax.sharding import PartitionSpec as P

HEADS = 64
KV_HEADS = 8
GROUP = HEADS // KV_HEADS
HD = 128
BLK = 32
PMAX = 384
QB = 128
NEG = -1e30
C2 = HD ** -0.5 * math.log2(math.e)
MESH = pl.DeviceIdType.MESH


def dot_nt(a, b):
    return lax.dot_general(a, b, (((1,), (1,)), ((), ())), preferred_element_type=jnp.float32)


def dot_tn(a, b):
    return lax.dot_general(a, b, (((0,), (0,)), ((), ())), preferred_element_type=jnp.float32)


def loop(lo, hi, body, carry):
    if hi - lo <= 4:
        for k in range(lo, hi):
            carry = body(k, carry)
        return carry
    return lax.fori_loop(lo, hi, body, carry)


def each(lo, hi, body):
    def step(k, carry):
        body(k)
        return carry

    loop(lo, hi, step, 0)


def kernel(
    n, m,
    pre_q, pre_kv, prompt_len, page_owner, page_row, dq, dec_kv, cache, cache_len, w_out,
    pre_out, dec_out,
    pq, pkv, ckv, w, ob,
    pk, pv, ck, cv, gid, bias, sl,
    qall, rpo, rml, spo, sml, aall, pf, pj, rp,
    lsem, osem, qs, qr, os_, or_, ms, mr, as_, ar, js, jr,
):
    me = lax.axis_index("inst")
    mt = lax.axis_index("tp")
    ptok = pre_q.shape[0]
    nh = pre_kv.shape[2] // HD
    rdev, cap = cache.shape[0], cache.shape[1]
    rows = dq.shape[0]
    steps = rows // rdev
    qv = GROUP * rows
    pages = ptok // BLK

    loads = [
        pltpu.make_async_copy(src, dst, lsem.at[i])
        for i, (src, dst) in enumerate(((cache, ckv), (pre_kv, pkv), (pre_q, pq), (w_out, w)))
    ]
    for c in loads:
        c.start()

    barrier = pltpu.get_barrier_semaphore()
    each(1, n, lambda k: pl.semaphore_signal(
        barrier, inc=1, device_id={"inst": lax.rem(me + k, n)}, device_id_type=MESH))
    each(1, m, lambda k: pl.semaphore_signal(
        barrier, inc=1, device_id={"tp": lax.rem(mt + k, m)}, device_id_type=MESH))
    pl.semaphore_wait(barrier, n + m - 2)

    def q_copy(k):
        return pltpu.make_async_remote_copy(
            src_ref=dq, dst_ref=qall.at[k], send_sem=qs.at[k], recv_sem=qr.at[k],
            device_id={"inst": lax.rem(me + k, n)}, device_id_type=MESH)

    def o_copy(k):
        return pltpu.make_async_remote_copy(
            src_ref=spo.at[k], dst_ref=rpo.at[k], send_sem=os_.at[k], recv_sem=or_.at[k],
            device_id={"inst": lax.rem(me - k + n, n)}, device_id_type=MESH)

    def m_copy(k):
        return pltpu.make_async_remote_copy(
            src_ref=sml.at[k], dst_ref=rml.at[k], send_sem=ms.at[k], recv_sem=mr.at[k],
            device_id={"inst": lax.rem(me - k + n, n)}, device_id_type=MESH)

    def a_copy(k, owner):
        block = aall.at[pl.ds(pl.multiple_of(owner * rows, rows), rows)]
        return pltpu.make_async_remote_copy(
            src_ref=block, dst_ref=block, send_sem=as_.at[k], recv_sem=ar.at[k],
            device_id={"inst": lax.rem(me + k, n)}, device_id_type=MESH)

    rpt = n * rows // m

    def j_copy(k):
        dest = lax.rem(mt + k, m)
        return pltpu.make_async_remote_copy(
            src_ref=pj.at[pl.ds(pl.multiple_of(dest * rpt, rpt), rpt)], dst_ref=rp.at[k],
            send_sem=js.at[k], recv_sem=jr.at[k], device_id={"tp": dest}, device_id_type=MESH)

    each(1, n, lambda k: q_copy(k).start())

    lane = lax.broadcasted_iota(jnp.int32, (1, qv), 1)
    lane_row = lax.rem(lane, rows) // steps
    lane_step = lax.rem(lane, steps)

    def stacked(ref, h):
        return jnp.concatenate(
            [ref[:, (h * GROUP + g) * HD:(h * GROUP + g + 1) * HD] for g in range(GROUP)], axis=0)

    loads[0].wait()
    chunk = 256
    for h in range(nh):
        cols = slice(h * HD, (h + 1) * HD)

        def split(j, carry, h=h, cols=cols):
            r, t = j // (cap // chunk), lax.rem(j, cap // chunk) * chunk
            at = pl.multiple_of(j * chunk, chunk)
            ck[h, pl.ds(at, chunk), :] = ckv[r, pl.ds(t, chunk), 0, cols]
            cv[h, pl.ds(at, chunk), :] = ckv[r, pl.ds(t, chunk), 1, cols]
            return carry

        lax.fori_loop(0, rdev * cap // chunk, split, 0)
        ck[h, rdev * cap:, :] = dec_kv[:, 0, cols]
        cv[h, rdev * cap:, :] = dec_kv[:, 1, cols]

    local = []
    slot = lax.broadcasted_iota(jnp.int32, (cap, qv), 0)
    fresh = lax.broadcasted_iota(jnp.int32, (rows, qv), 0)
    for h in range(nh):
        query = stacked(dq, h)
        best = jnp.full((1, qv), NEG, jnp.float32)
        for r in range(rdev):
            s = dot_nt(ck[h, r * cap:(r + 1) * cap, :], query)
            s = jnp.where((slot < cache_len[0, r]) & (lane_row == r), s, NEG)
            sl[r * cap:(r + 1) * cap, :] = s
            best = jnp.maximum(best, jnp.max(s, axis=0, keepdims=True))
        s = dot_nt(ck[h, rdev * cap:, :], query)
        s = jnp.where((fresh // steps == lane_row) & (lax.rem(fresh, steps) <= lane_step), s, NEG)
        sl[rdev * cap:, :] = s
        best = jnp.maximum(best, jnp.max(s, axis=0, keepdims=True))
        total = jnp.zeros((1, qv), jnp.float32)
        mixed = jnp.zeros((HD, qv), jnp.float32)
        for r in range(rdev + 1):
            at = slice(r * cap, min((r + 1) * cap, rdev * cap + rows))
            p = jnp.exp2((sl[at, :] - best) * C2)
            total = total + jnp.sum(p, axis=0, keepdims=True)
            mixed = mixed + dot_tn(cv[h, at, :], p.astype(jnp.bfloat16))
        local.append((best, total, mixed))

    loads[1].wait()
    for h in range(nh):
        cols = slice(h * HD, (h + 1) * HD)

        def part(j, carry, h=h, cols=cols):
            t = pl.multiple_of(j * chunk, chunk)
            pk[h, pl.ds(t, chunk), :] = pkv[pl.ds(t, chunk), 0, cols]
            pv[h, pl.ds(t, chunk), :HD] = pkv[pl.ds(t, chunk), 1, cols]
            pv[h, pl.ds(t, chunk), HD:] = jnp.ones((chunk, HD), jnp.bfloat16)
            return carry

        lax.fori_loop(0, ptok // chunk, part, 0)
    for p in range(pages):
        at = me * pages + p
        gid[p * BLK:(p + 1) * BLK, :] = jnp.full(
            (BLK, qv), page_owner[at] * rdev + page_row[at], jnp.int32)

    def page_part(k, q_ref, o_ref, m_ref):
        owner = lax.rem(me - k + n, n)
        mine = gid[...] == owner * rdev + lane_row
        for h in range(nh):
            s = dot_nt(pk[h], stacked(q_ref, h))
            s = jnp.where(mine, s, NEG)
            best = jnp.max(s, axis=0, keepdims=True)
            p = jnp.where(mine, jnp.exp2((s - best) * C2), 0.0)
            m_ref[2 * h:2 * h + 1, :] = best
            m_ref[2 * h + 1:2 * h + 2, :] = jnp.sum(p, axis=0, keepdims=True)
            o_ref[h] = dot_tn(pv[h, :, :HD], p.astype(jnp.bfloat16)).astype(jnp.bfloat16)

    def remote_part(k, carry):
        q_copy(k).wait_recv()
        page_part(k, qall.at[k], spo.at[k], sml.at[k])
        o_copy(k).start()
        m_copy(k).start()
        return carry

    lax.fori_loop(1, n, remote_part, 0)
    page_part(0, dq, rpo.at[0], rml.at[0])

    def prefill(h, blocks):
        for i in blocks:
            lo, hi = max(0, i - PMAX // QB) * QB, (i + 1) * QB
            wide = hi - lo
            token = lax.broadcasted_iota(jnp.int32, (QB, HD), 0) + i * QB
            first = jnp.zeros((QB, HD), jnp.int32)
            end = 0
            for j in range(prompt_len.shape[1]):
                length = prompt_len[0, j]
                end = end + length
                first = jnp.where(token >= end, first + length, first)
            for b in range(wide // HD):
                key = lax.broadcasted_iota(jnp.int32, (QB, HD), 1) + (lo + b * HD)
                bias[:, b * HD:(b + 1) * HD] = jnp.where(
                    (key >= first) & (key <= token), 0.0, NEG)

            def head(g, carry):
                at = pl.multiple_of((h * GROUP + g) * HD, HD)
                s = dot_nt(pq[i * QB:(i + 1) * QB, pl.ds(at, HD)], pk[h, lo:hi, :])
                s = s + bias[:, :wide]
                best = jnp.max(s, axis=1, keepdims=True)
                p = jnp.exp2((s - best) * C2).astype(jnp.bfloat16)
                o = jnp.dot(p, pv[h, lo:hi, :], preferred_element_type=jnp.float32)
                ob[i * QB:(i + 1) * QB, pl.ds(at, HD)] = (o[:, :HD] / o[:, HD:]).astype(jnp.bfloat16)
                return carry

            lax.fori_loop(0, GROUP, head, 0, unroll=2)

    blocks = ptok // QB
    work = [(h, i) for h in range(nh) for i in range(blocks)]
    cut1, cut2 = len(work) * 5 // 12, len(work) * 10 // 12

    def out_copy(i):
        return pltpu.make_async_copy(
            ob.at[i * QB:(i + 1) * QB], pre_out.at[i * QB:(i + 1) * QB], osem.at[i])

    def do(items):
        for h, i in items:
            prefill(h, [i])
            if h == nh - 1:
                out_copy(i).start()

    loads[2].wait()
    do(work[:cut1])

    each(1, n, lambda k: (o_copy(k).wait_recv(), m_copy(k).wait_recv()))
    for h in range(nh):
        best0, total0, mixed0 = local[h]
        best = loop(0, n, lambda k, b: jnp.maximum(b, rml[k, 2 * h:2 * h + 1, :]), best0)
        f0 = jnp.exp2((best0 - best) * C2)

        def add(k, carry):
            total, mixed = carry
            f = jnp.exp2((rml[k, 2 * h:2 * h + 1, :] - best) * C2)
            return (total + f * rml[k, 2 * h + 1:2 * h + 2, :],
                    mixed + f * rpo[k, h].astype(jnp.float32))

        total, mixed = loop(0, n, add, (total0 * f0, mixed0 * f0))
        att = jnp.transpose(mixed / total).astype(jnp.bfloat16)
        for g in range(GROUP):
            c = (h * GROUP + g) * HD
            aall[pl.ds(pl.multiple_of(me * rows, rows), rows), c:c + HD] = att[g * rows:(g + 1) * rows]
    each(1, n, lambda k: a_copy(k, me).start())

    do(work[cut1:cut2])

    loads[3].wait()
    each(1, n, lambda k: a_copy(k, lax.rem(me - k + n, n)).wait_recv())
    wide = w.shape[1]
    piece = min(512, wide)

    def project(j, carry):
        c = pl.ds(pl.multiple_of(j * piece, piece), piece)
        acc = jnp.dot(aall[...], w[:, c], preferred_element_type=jnp.float32)
        pf[:, c] = acc
        pj[:, c] = acc.astype(jnp.bfloat16)
        return carry

    lax.fori_loop(0, wide // piece, project, 0)
    each(1, m, lambda k: j_copy(k).start())

    do(work[cut2:])

    each(1, m, lambda k: j_copy(k).wait_recv())
    acc = loop(1, m, lambda k, a: a + rp[k].astype(jnp.float32),
               pf[pl.ds(pl.multiple_of(mt * rpt, rpt), rpt), :])
    dec_out[...] = acc.astype(jnp.bfloat16)

    each(1, n, lambda k: (q_copy(k).wait_send(), o_copy(k).wait_send(),
                          m_copy(k).wait_send(), a_copy(k, me).wait_send()))
    each(1, m, lambda k: j_copy(k).wait_send())
    for i in range(blocks):
        out_copy(i).wait()


def local(pre_q, pre_kv, prompt_len, page_owner, page_row, dec_q, dec_kv, cache_kv, cache_len, w_out):
    n, m = lax.axis_size("inst"), lax.axis_size("tp")
    ptok, width = pre_q.shape
    nh = pre_kv.shape[2] // HD
    rdev, steps = dec_q.shape[0], dec_q.shape[1]
    rows = rdev * steps
    qv = GROUP * rows
    slots = rdev * cache_kv.shape[1] + rows
    bf, f32 = jnp.bfloat16, jnp.float32
    any_, vmem, smem = (pl.BlockSpec(memory_space=s) for s in (pl.ANY, pltpu.VMEM, pltpu.SMEM))
    outw = w_out.shape[1]
    rpt = n * rows // m
    dma = pltpu.SemaphoreType.DMA
    return pl.pallas_call(
        functools.partial(kernel, n, m),
        out_shape=(jax.ShapeDtypeStruct((ptok, width), bf), jax.ShapeDtypeStruct((rpt, outw), bf)),
        in_specs=[any_, any_, smem, smem, smem, vmem, vmem, any_, smem, any_],
        out_specs=(any_, vmem),
        scratch_shapes=[
            pltpu.VMEM(pre_q.shape, bf), pltpu.VMEM(pre_kv.shape, bf), pltpu.VMEM(cache_kv.shape, bf),
            pltpu.VMEM(w_out.shape, bf), pltpu.VMEM((ptok, width), bf),
            pltpu.VMEM((nh, ptok, HD), bf), pltpu.VMEM((nh, ptok, 2 * HD), bf),
            pltpu.VMEM((nh, slots, HD), bf), pltpu.VMEM((nh, slots, HD), bf),
            pltpu.VMEM((ptok, qv), jnp.int32), pltpu.VMEM((QB, PMAX + QB), f32), pltpu.VMEM((slots, qv), f32),
            pltpu.VMEM((n, rows, width), bf),
            pltpu.VMEM((n, nh, HD, qv), bf), pltpu.VMEM((n, 8, qv), f32),
            pltpu.VMEM((n, nh, HD, qv), bf), pltpu.VMEM((n, 8, qv), f32),
            pltpu.VMEM((n * rows, width), bf), pltpu.VMEM((n * rows, outw), f32),
            pltpu.VMEM((n * rows, outw), bf), pltpu.VMEM((m, rpt, outw), bf),
            dma((4,)), dma((ptok // QB,)),
            dma((n,)), dma((n,)), dma((n,)), dma((n,)), dma((n,)), dma((n,)), dma((n,)), dma((n,)),
            dma((m,)), dma((m,)),
        ],
        compiler_params=pltpu.CompilerParams(
            collective_id=0, has_side_effects=True, vmem_limit_bytes=56 << 20),
    )(pre_q, pre_kv, prompt_len, page_owner.reshape(-1), page_row,
      dec_q.reshape(rows, width), dec_kv.reshape((rows,) + dec_kv.shape[2:]), cache_kv, cache_len, w_out)


def solution(mesh):
    return jax.shard_map(
        local,
        mesh=mesh,
        in_specs=(
            P(("grp", "inst"), "tp"),
            P(("grp", "inst"), None, "tp"),
            P(("grp", "inst"), None),
            P("grp", None),
            P("grp"),
            P(("grp", "inst"), None, "tp"),
            P(("grp", "inst"), None, None, "tp"),
            P(("grp", "inst"), None, None, "tp"),
            P(("grp", "inst"), None),
            P("tp", "inst"),
        ),
        out_specs=(P(("grp", "inst"), "tp"), P(("grp", "tp"), "inst")),
        check_vma=False,
    )
```

```python
import functools
import math

import jax
import jax.numpy as jnp
from jax import lax
from jax.experimental import pallas as pl
from jax.experimental.pallas import tpu as pltpu
from jax.sharding import PartitionSpec as P

HEADS = 64
KV_HEADS = 8
GROUP = HEADS // KV_HEADS
HD = 128
BLK = 32
PMAX = 384
QB = 128
NEG = -1e30
C2 = HD ** -0.5 * math.log2(math.e)
MESH = pl.DeviceIdType.MESH


def dot_nt(a, b):
    return lax.dot_general(a, b, (((1,), (1,)), ((), ())), preferred_element_type=jnp.float32)


def dot_tn(a, b):
    return lax.dot_general(a, b, (((0,), (0,)), ((), ())), preferred_element_type=jnp.float32)


def loop(lo, hi, body, carry):
    if hi - lo <= 4:
        for k in range(lo, hi):
            carry = body(k, carry)
        return carry
    return lax.fori_loop(lo, hi, body, carry)


def each(lo, hi, body):
    def step(k, carry):
        body(k)
        return carry

    loop(lo, hi, step, 0)


def kernel(
    n, m,
    pre_q, pre_kv, prompt_len, page_owner, page_row, dq, dec_kv, cache, cache_len, w_out,
    pre_out, dec_out,
    pq, pkv, ckv, w, ob,
    pk, pv, ck, cv, gid, bias, sl,
    qall, rpo, rml, spo, sml, aall, pf, pj, rp,
    lsem, osem, qs, qr, os_, or_, ms, mr, as_, ar, js, jr,
):
    me = lax.axis_index("inst")
    mt = lax.axis_index("tp")
    ptok = pre_q.shape[0]
    nh = pre_kv.shape[2] // HD
    rdev, cap = cache.shape[0], cache.shape[1]
    steps = dq.shape[1]
    rows = rdev * steps
    qv = GROUP * rows
    pages = ptok // BLK

    loads = [
        pltpu.make_async_copy(src, dst, lsem.at[i])
        for i, (src, dst) in enumerate(((cache, ckv), (pre_kv, pkv), (pre_q, pq), (w_out, w)))
    ]
    for c in loads:
        c.start()

    barrier = pltpu.get_barrier_semaphore()
    each(1, n, lambda k: pl.semaphore_signal(
        barrier, inc=1, device_id={"inst": lax.rem(me + k, n)}, device_id_type=MESH))
    each(1, m, lambda k: pl.semaphore_signal(
        barrier, inc=1, device_id={"tp": lax.rem(mt + k, m)}, device_id_type=MESH))

    def q_copy(k):
        return pltpu.make_async_remote_copy(
            src_ref=dq, dst_ref=qall.at[k], send_sem=qs.at[k], recv_sem=qr.at[k],
            device_id={"inst": lax.rem(me + k, n)}, device_id_type=MESH)

    def o_copy(k):
        return pltpu.make_async_remote_copy(
            src_ref=spo.at[k], dst_ref=rpo.at[k], send_sem=os_.at[k], recv_sem=or_.at[k],
            device_id={"inst": lax.rem(me - k + n, n)}, device_id_type=MESH)

    def m_copy(k):
        return pltpu.make_async_remote_copy(
            src_ref=sml.at[k], dst_ref=rml.at[k], send_sem=ms.at[k], recv_sem=mr.at[k],
            device_id={"inst": lax.rem(me - k + n, n)}, device_id_type=MESH)

    def a_copy(k, owner):
        block = aall.at[pl.ds(pl.multiple_of(owner * rows, rows), rows)]
        return pltpu.make_async_remote_copy(
            src_ref=block, dst_ref=block, send_sem=as_.at[k], recv_sem=ar.at[k],
            device_id={"inst": lax.rem(me + k, n)}, device_id_type=MESH)

    rpt = n * rows // m

    def j_copy(k):
        dest = lax.rem(mt + k, m)
        return pltpu.make_async_remote_copy(
            src_ref=pj.at[pl.ds(pl.multiple_of(dest * rpt, rpt), rpt)], dst_ref=rp.at[k],
            send_sem=js.at[k], recv_sem=jr.at[k], device_id={"tp": dest}, device_id_type=MESH)

    lane = lax.broadcasted_iota(jnp.int32, (1, qv), 1)
    lane_row = lax.rem(lane, rows) // steps
    lane_step = lax.rem(lane, steps)

    def stacked(ref, h):
        return jnp.concatenate(
            [ref[:, :, (h * GROUP + g) * HD:(h * GROUP + g + 1) * HD].reshape(rows, HD)
             for g in range(GROUP)], axis=0)

    loads[0].wait()
    chunk = 256
    for h in range(nh):
        cols = slice(h * HD, (h + 1) * HD)

        def split(j, carry, h=h, cols=cols):
            r, t = j // (cap // chunk), lax.rem(j, cap // chunk) * chunk
            at = pl.multiple_of(j * chunk, chunk)
            ck[h, pl.ds(at, chunk), :] = ckv[r, pl.ds(t, chunk), 0, cols]
            cv[h, pl.ds(at, chunk), :] = ckv[r, pl.ds(t, chunk), 1, cols]
            return carry

        lax.fori_loop(0, rdev * cap // chunk, split, 0)
        ck[h, rdev * cap:, :] = dec_kv[:, 0, cols]
        cv[h, rdev * cap:, :] = dec_kv[:, 1, cols]

    local = []
    slot = lax.broadcasted_iota(jnp.int32, (cap, qv), 0)
    fresh = lax.broadcasted_iota(jnp.int32, (rows, qv), 0)
    for h in range(nh):
        query = stacked(dq, h)
        best = jnp.full((1, qv), NEG, jnp.float32)
        for r in range(rdev):
            s = dot_nt(ck[h, r * cap:(r + 1) * cap, :], query)
            s = jnp.where((slot < cache_len[0, r]) & (lane_row == r), s, NEG)
            sl[r * cap:(r + 1) * cap, :] = s
            best = jnp.maximum(best, jnp.max(s, axis=0, keepdims=True))
        s = dot_nt(ck[h, rdev * cap:, :], query)
        s = jnp.where((fresh // steps == lane_row) & (lax.rem(fresh, steps) <= lane_step), s, NEG)
        sl[rdev * cap:, :] = s
        best = jnp.maximum(best, jnp.max(s, axis=0, keepdims=True))
        total = jnp.zeros((1, qv), jnp.float32)
        mixed = jnp.zeros((HD, qv), jnp.float32)
        for r in range(rdev + 1):
            at = slice(r * cap, min((r + 1) * cap, rdev * cap + rows))
            p = jnp.exp2((sl[at, :] - best) * C2)
            total = total + jnp.sum(p, axis=0, keepdims=True)
            mixed = mixed + dot_tn(cv[h, at, :], p.astype(jnp.bfloat16))
        local.append((best, total, mixed))

    loads[1].wait()
    for h in range(nh):
        cols = slice(h * HD, (h + 1) * HD)

        def part(j, carry, h=h, cols=cols):
            t = pl.multiple_of(j * chunk, chunk)
            pk[h, pl.ds(t, chunk), :] = pkv[pl.ds(t, chunk), 0, cols]
            pv[h, pl.ds(t, chunk), :HD] = pkv[pl.ds(t, chunk), 1, cols]
            pv[h, pl.ds(t, chunk), HD:] = jnp.ones((chunk, HD), jnp.bfloat16)
            return carry

        lax.fori_loop(0, ptok // chunk, part, 0)
    for p in range(pages):
        at = me * pages + p
        gid[p * BLK:(p + 1) * BLK, :] = jnp.full(
            (BLK, qv), page_owner[at] * rdev + page_row[at], jnp.int32)

    def page_part(k, q_ref, o_ref, m_ref):
        owner = lax.rem(me - k + n, n)
        mine = gid[...] == owner * rdev + lane_row
        for h in range(nh):
            s = dot_nt(pk[h], stacked(q_ref, h))
            s = jnp.where(mine, s, NEG)
            best = jnp.max(s, axis=0, keepdims=True)
            p = jnp.where(mine, jnp.exp2((s - best) * C2), 0.0)
            m_ref[2 * h:2 * h + 1, :] = best
            m_ref[2 * h + 1:2 * h + 2, :] = jnp.sum(p, axis=0, keepdims=True)
            o_ref[h] = dot_tn(pv[h, :, :HD], p.astype(jnp.bfloat16)).astype(jnp.bfloat16)

    def prefill(h, blocks):
        for i in blocks:
            lo, hi = max(0, i - PMAX // QB) * QB, (i + 1) * QB
            wide = hi - lo
            token = lax.broadcasted_iota(jnp.int32, (QB, HD), 0) + i * QB
            first = jnp.zeros((QB, HD), jnp.int32)
            end = 0
            for j in range(prompt_len.shape[1]):
                length = prompt_len[0, j]
                end = end + length
                first = jnp.where(token >= end, first + length, first)
            for b in range(wide // HD):
                key = lax.broadcasted_iota(jnp.int32, (QB, HD), 1) + (lo + b * HD)
                bias[:, b * HD:(b + 1) * HD] = jnp.where(
                    (key >= first) & (key <= token), 0.0, NEG)

            def head(g, carry):
                at = pl.multiple_of((h * GROUP + g) * HD, HD)
                s = dot_nt(pq[i * QB:(i + 1) * QB, pl.ds(at, HD)], pk[h, lo:hi, :])
                s = s + bias[:, :wide]
                best = jnp.max(s, axis=1, keepdims=True)
                p = jnp.exp2((s - best) * C2).astype(jnp.bfloat16)
                o = jnp.dot(p, pv[h, lo:hi, :], preferred_element_type=jnp.float32)
                ob[i * QB:(i + 1) * QB, pl.ds(at, HD)] = (o[:, :HD] / o[:, HD:]).astype(jnp.bfloat16)
                return carry

            lax.fori_loop(0, GROUP, head, 0, unroll=GROUP)

    blocks = ptok // QB
    stages = [[], [blocks - 1, 0], [blocks - 2, blocks - 3], list(range(blocks - 4, 0, -1))]

    def out_copy(i):
        return pltpu.make_async_copy(
            ob.at[i * QB:(i + 1) * QB], pre_out.at[i * QB:(i + 1) * QB], osem.at[i])

    def do(stage):
        for i in stages[stage]:
            for h in range(nh):
                prefill(h, [i])
            out_copy(i).start()

    loads[2].wait()
    do(0)
    pl.semaphore_wait(barrier, n + m - 2)
    each(1, n, lambda k: q_copy(k).start())
    do(1)

    def remote_part(k, carry):
        q_copy(k).wait_recv()
        page_part(k, qall.at[k], spo.at[k], sml.at[k])
        o_copy(k).start()
        m_copy(k).start()
        return carry

    lax.fori_loop(1, n, remote_part, 0)
    page_part(0, dq, rpo.at[0], rml.at[0])

    do(2)

    each(1, n, lambda k: (o_copy(k).wait_recv(), m_copy(k).wait_recv()))
    for h in range(nh):
        best0, total0, mixed0 = local[h]
        best = loop(0, n, lambda k, b: jnp.maximum(b, rml[k, 2 * h:2 * h + 1, :]), best0)
        f0 = jnp.exp2((best0 - best) * C2)

        def add(k, carry):
            total, mixed = carry
            f = jnp.exp2((rml[k, 2 * h:2 * h + 1, :] - best) * C2)
            return (total + f * rml[k, 2 * h + 1:2 * h + 2, :],
                    mixed + f * rpo[k, h].astype(jnp.float32))

        total, mixed = loop(0, n, add, (total0 * f0, mixed0 * f0))
        att = jnp.transpose(mixed / total).astype(jnp.bfloat16)
        for g in range(GROUP):
            c = (h * GROUP + g) * HD
            aall[pl.ds(pl.multiple_of(me * rows, rows), rows), c:c + HD] = att[g * rows:(g + 1) * rows]
    each(1, n, lambda k: a_copy(k, me).start())

    do(3)

    loads[3].wait()
    each(1, n, lambda k: a_copy(k, lax.rem(me - k + n, n)).wait_recv())
    wide = w.shape[1]
    piece = min(512, wide)

    def project(j, carry):
        c = pl.ds(pl.multiple_of(j * piece, piece), piece)
        acc = jnp.dot(aall[...], w[:, c], preferred_element_type=jnp.float32)
        pf[:, c] = acc
        pj[:, c] = acc.astype(jnp.bfloat16)
        return carry

    lax.fori_loop(0, wide // piece, project, 0)
    each(1, m, lambda k: j_copy(k).start())

    each(1, m, lambda k: j_copy(k).wait_recv())
    acc = loop(1, m, lambda k, a: a + rp[k].astype(jnp.float32),
               pf[pl.ds(pl.multiple_of(mt * rpt, rpt), rpt), :])
    dec_out[...] = acc.astype(jnp.bfloat16)

    each(1, n, lambda k: (q_copy(k).wait_send(), o_copy(k).wait_send(),
                          m_copy(k).wait_send(), a_copy(k, me).wait_send()))
    each(1, m, lambda k: j_copy(k).wait_send())
    for i in range(blocks):
        out_copy(i).wait()


def local(pre_q, pre_kv, prompt_len, page_owner, page_row, dec_q, dec_kv, cache_kv, cache_len, w_out):
    n, m = lax.axis_size("inst"), lax.axis_size("tp")
    ptok, width = pre_q.shape
    nh = pre_kv.shape[2] // HD
    rdev, steps = dec_q.shape[0], dec_q.shape[1]
    rows = rdev * steps
    qv = GROUP * rows
    slots = rdev * cache_kv.shape[1] + rows
    bf, f32 = jnp.bfloat16, jnp.float32
    any_, vmem, smem = (pl.BlockSpec(memory_space=s) for s in (pl.ANY, pltpu.VMEM, pltpu.SMEM))
    outw = w_out.shape[1]
    rpt = n * rows // m
    dma = pltpu.SemaphoreType.DMA
    return pl.pallas_call(
        functools.partial(kernel, n, m),
        out_shape=(jax.ShapeDtypeStruct((ptok, width), bf), jax.ShapeDtypeStruct((rpt, outw), bf)),
        in_specs=[any_, any_, smem, smem, smem, vmem, vmem, any_, smem, any_],
        out_specs=(any_, vmem),
        scratch_shapes=[
            pltpu.VMEM(pre_q.shape, bf), pltpu.VMEM(pre_kv.shape, bf), pltpu.VMEM(cache_kv.shape, bf),
            pltpu.VMEM(w_out.shape, bf), pltpu.VMEM((ptok, width), bf),
            pltpu.VMEM((nh, ptok, HD), bf), pltpu.VMEM((nh, ptok, 2 * HD), bf),
            pltpu.VMEM((nh, slots, HD), bf), pltpu.VMEM((nh, slots, HD), bf),
            pltpu.VMEM((ptok, qv), jnp.int32), pltpu.VMEM((QB, PMAX + QB), f32), pltpu.VMEM((slots, qv), f32),
            pltpu.VMEM((n,) + dec_q.shape, bf),
            pltpu.VMEM((n, nh, HD, qv), bf), pltpu.VMEM((n, 8, qv), f32),
            pltpu.VMEM((n, nh, HD, qv), bf), pltpu.VMEM((n, 8, qv), f32),
            pltpu.VMEM((n * rows, width), bf), pltpu.VMEM((n * rows, outw), f32),
            pltpu.VMEM((n * rows, outw), bf), pltpu.VMEM((m, rpt, outw), bf),
            dma((4,)), dma((ptok // QB,)),
            dma((n,)), dma((n,)), dma((n,)), dma((n,)), dma((n,)), dma((n,)), dma((n,)), dma((n,)),
            dma((m,)), dma((m,)),
        ],
        compiler_params=pltpu.CompilerParams(
            collective_id=0, has_side_effects=True, vmem_limit_bytes=56 << 20),
    )(pre_q, pre_kv, prompt_len, page_owner.reshape(-1), page_row,
      dec_q, dec_kv.reshape((rows,) + dec_kv.shape[2:]), cache_kv, cache_len, w_out)


def solution(mesh):
    return jax.shard_map(
        local,
        mesh=mesh,
        in_specs=(
            P(("grp", "inst"), "tp"),
            P(("grp", "inst"), None, "tp"),
            P(("grp", "inst"), None),
            P("grp", None),
            P("grp"),
            P(("grp", "inst"), None, "tp"),
            P(("grp", "inst"), None, None, "tp"),
            P(("grp", "inst"), None, None, "tp"),
            P(("grp", "inst"), None),
            P("tp", "inst"),
        ),
        out_specs=(P(("grp", "inst"), "tp"), P(("grp", "tp"), "inst")),
        check_vma=False,
    )
```
